256 devices in a mesh: dp: 16 (over y_lo, z), factor: 16 (over x, y_hi, core).
Axes of the slice: x: 4, y: 4 (y_hi: 2, y_lo: 2; y = y_hi * 2 + y_lo), z: 8, core: 2. Of those that a mesh axis runs over, the one named last changes fastest.
Arguments:
- train_inputs: bfloat16 [128, 8, 64, 320], P('dp'), may hold values from -6 to 6
- train_cotangents: bfloat16 [128, 8, 64, 320], P('dp'), may hold values from -0.26367188 to 0.26367188
- query_inputs: bfloat16 [16, 8, 64, 320], P('dp'), may hold values from -6 to 6
- query_cotangents: bfloat16 [16, 8, 64, 320], P('dp'), may hold values from -0.26367188 to 0.26367188
- timesteps: int32 [128], P('dp'), may hold values from 0 to 999
- input_basis: bfloat16 [2880, 2880], P('dp', 'factor'), may hold values from -0.109375 to 0.109375
- output_basis: bfloat16 [320, 320], replicated, may hold values from -0.3125 to 0.3125
- eigenvalues: float32 [320, 2880], P(None, 'factor'), may hold values from 0.1 to 10
Outputs:
- scores: float32 [128], P('dp')
- query_proj: float32 [320, 2880], P(None, 'factor')
The draws below stay inside these ranges and needn't reach their ends.
All inputs are finite; a program needn't handle non-finite values.
Results may differ from the reference program's by a relative error of at most 0.0037.
Values may be sent and summed in bfloat16 or wider, within the bound.
A program may use at most 192 MiB of HBM per device.

```python
import math
import jax
import jax.numpy as jnp
from jax import lax

C = 320
K = 2880
IMG_W = 64
ROWS = 8
POSITIONS = 512
TRAIN = 128
QUERIES = 16


def set_ends(values, key, least, high):
    longest = values.shape.index(max(values.shape))
    spots = []
    for shift in (0, 1):
        where = [jax.random.randint(jax.random.fold_in(key, axis), (), 0, length) for axis, length in enumerate(values.shape)]
        where[longest] = (where[longest] + shift) % values.shape[longest]
        spots.append(tuple(where))
    return values.at[spots[0]].set(least).at[spots[1]].set(high)


def levels(key, dims, shards, least, largest):
    level, own = 1.0, jax.random.fold_in(key, 6)
    for axis_at, parts in shards:
        draws = jnp.exp(jax.random.uniform(jax.random.fold_in(own, axis_at), (parts,), jnp.float32, least / len(shards), largest / len(shards)))
        level = level * jnp.repeat(draws, dims[axis_at] // parts).reshape([-1 if axis == axis_at else 1 for axis in range(len(dims))])
    return level


def normal_values(own_key, dims, spread, reach, cuts=(), held_as=jnp.bfloat16):
    array = jax.random.normal(own_key, dims, jnp.float32) * spread
    if len(cuts) > 0:
        array = levels(own_key, dims, cuts, -0.22, 0.18) * array
    return jnp.clip(array, min=-reach, max=reach).astype(held_as)


def setup_inputs(seed: int = 0) -> dict:
    keys = jax.random.split(jax.random.key(seed), 9)
    return {
        "train_inputs": normal_values(keys[0], (TRAIN, ROWS, IMG_W, C), 1.0, 6.0, ((0, 16),)),
        "train_cotangents": normal_values(keys[1], (TRAIN, ROWS, IMG_W, C), (POSITIONS ** -0.5), 0.26367188, ((0, 16),)),
        "query_inputs": normal_values(keys[2], (QUERIES, ROWS, IMG_W, C), 1.0, 6.0, ((0, 16),)),
        "query_cotangents": normal_values(keys[3], (QUERIES, ROWS, IMG_W, C), (POSITIONS ** -0.5), 0.26367188, ((0, 16),)),
        "timesteps": set_ends(jax.random.randint(keys[4], (TRAIN,), 0, 1000), jax.random.fold_in(keys[4], 1), 0, 999).astype(jnp.int32),
        "input_basis": normal_values(keys[5], (K, K), K ** -0.5, 0.109375, ((0, 16), (1, 16))),
        "output_basis": normal_values(keys[6], (C, C), C ** -0.5, 0.3125),
        "eigenvalues": jnp.clip(jnp.exp(math.log(10.0) - 4.6051702 * jax.random.uniform(keys[7], (C, K), jnp.float32) ** levels(keys[7], (C, K), ((1, 16),), -0.2, 0.2)), 0.1, 10.0),
    }


def patch_matrix(activations):
    rows_count, cols_count, channels = activations.shape
    padded = jnp.pad(activations, ((1, 1), (1, 1), (0, 0)))
    taps = [padded[row_off:row_off + rows_count, col_off:col_off + cols_count, :] for row_off in range(3) for col_off in range(3)]
    return jnp.concatenate(taps, axis=-1).reshape(rows_count * cols_count, 9 * channels)

def reference(train_inputs, train_cotangents, query_inputs, query_cotangents, timesteps, input_basis, output_basis, eigenvalues):
    high = lax.Precision.HIGHEST
    basis_in = input_basis.astype(jnp.float32)
    basis_out = output_basis.astype(jnp.float32)
    channels = output_basis.shape[0]
    width = input_basis.shape[0]

    def one_query(pair):
        inputs, cotangents = pair
        patches = patch_matrix(inputs).astype(jnp.float32)
        return jnp.dot(cotangents.reshape(-1, channels).astype(jnp.float32).T, patches, precision=high)
    query_grad = lax.optimization_barrier(jnp.sum(lax.map(one_query, (query_inputs, query_cotangents)), axis=0)) / QUERIES
    query_right = jnp.dot(query_grad, basis_in, precision=high)
    query_proj = jnp.dot(basis_out.T, query_right, precision=high) / (eigenvalues + 0.01)

    def one_train(pair):
        inputs, cotangents = pair
        patches = patch_matrix(inputs).astype(jnp.float32)
        projected = jnp.dot(patches, basis_in, precision=high).astype(jnp.bfloat16)
        rotated = jnp.dot(cotangents.reshape(-1, channels), output_basis, preferred_element_type=jnp.float32).astype(jnp.bfloat16)
        train_proj = jnp.dot(rotated.T, projected, preferred_element_type=jnp.float32)
        return jnp.sum(train_proj * query_proj)
    raw_scores = lax.map(one_train, (train_inputs, train_cotangents))
    phase = (timesteps.astype(jnp.float32) / 1000.0 + 0.008) / 1.008 * (math.pi / 2)
    weight = jnp.sin(phase)
    scores = raw_scores * weight / math.sqrt(channels * width)
    return (scores, query_proj)
```

```python
import functools
import math

import jax
import jax.numpy as jnp
from jax import lax
from jax.experimental import pallas as pl
from jax.experimental.pallas import tpu as pltpu
from jax.sharding import PartitionSpec as P

damping = 0.01
MESH = pl.DeviceIdType.MESH
bf16 = jnp.bfloat16
f32 = jnp.float32

NY, NZ = 2, 8
ND, NF = 16, 16
CH = 320
SIDE = 180
CS = 40
BLOCKS = 13
POS = 512
BATCH = 8
PREPARED = 5
PACK = 288

WHOLE, HALF_A, HALF_B = (0, 288), (0, 144), (144, 144)


def norm(origin):
    return (origin[0] % NY, origin[1] % NZ)


START = [
    ((0, 0), WHOLE, (0, 2)), ((0, 0), WHOLE, (0, -2)),
    ((0, 0), WHOLE, (0, 1)), ((0, 0), WHOLE, (0, -1)),
    ((0, 0), WHOLE, (1, 0)),
]
COLUMN = [
    ((0, -2), HALF_A, (0, 2)), ((0, 2), HALF_B, (0, -2)),
    ((0, -2), WHOLE, (0, 1)), ((0, 2), WHOLE, (0, -1)),
]
ACROSS_NEAR = [((0, k), WHOLE, (1, 0)) for k in (1, -1, 2, -2)]
ACROSS_FAR = [((0, k), WHOLE, (1, 0)) for k in (3, -3, 4)]
PLAN = START + COLUMN + ACROSS_NEAR + ACROSS_FAR
LANDS = {}
for number, (origin, rows, hop) in enumerate(PLAN):
    place = (norm((origin[0] - hop[0], origin[1] - hop[1])), rows)
    assert place not in LANDS
    LANDS[place] = number


DP_STEPS = sorted(
    ((dy, dz) for dy in range(NY) for dz in range(NZ) if dy or dz),
    key=lambda step: -(step[0] + min(step[1], NZ - step[1])),
)
FACTOR_STEPS = sorted(
    ((dx, dh, dc) for dx in range(4) for dh in range(2) for dc in range(2) if dx or dh or dc),
    key=lambda step: -(min(step[0], 4 - step[0]) + 2 * step[1] + 0.1 * step[2]),
)


def block_of(y, part):
    return jnp.where(part < BLOCKS - 1, part + 11 * y, 14 + 9 * y)


def fill_patches(raw, xl, slot):
    x = raw.reshape(POS, CH).astype(f32)
    col = lax.broadcasted_iota(jnp.int32, (POS, 1), 0) % 64
    main, rest = x[:, :256], x[:, 256:]
    zero_rest = jnp.zeros((POS, 64), f32)

    def left(v):
        return jnp.where(col == 0, 0.0, pltpu.roll(v, 1, 0))

    def right(v):
        return jnp.where(col == 63, 0.0, pltpu.roll(v, POS - 1, 0))

    wide = jnp.concatenate([rest, zero_rest], axis=1)
    swapped = pltpu.roll(wide, 64, 1)
    inside = pl.ds(64, POS)
    xl[slot, inside, 0:256] = left(main).astype(bf16)
    xl[slot, inside, 256:512] = main.astype(bf16)
    xl[slot, inside, 512:768] = right(main).astype(bf16)
    xl[slot, inside, 768:896] = (left(wide) + swapped).astype(bf16)
    xl[slot, inside, 896:1024] = right(wide).astype(bf16)


def kernel(
    x_hbm, cot_hbm, qx_hbm, qcot_hbm, bin_hbm, bout_hbm, eig_hbm, time_ref,
    score_ref, proj_hbm,
    x_raw, cot_raw, qx_raw, qcot_raw, bin_raw, bout, bout_t, eig_raw, scale,
    panels, flat, panel, xl, r_all, acc, w_all, proj_out,
    mq, p1_src, p1_dst, p2_buf, m_stack, ag_buf, v_flat, q_pad, ar_buf,
    load_sem, x_sem, cot_sem,
    bin_send, bin_recv, p1_send, p1_recv, p2_send, p2_recv, ag_send, ag_recv, ar_send, ar_recv,
):
    d = lax.axis_index("dp")
    f = lax.axis_index("factor")
    y, z = d // NZ, d % NZ
    fx, fh, fc = f // 4, f // 2 % 2, f % 2

    def dp_at(k, sign=1):
        dy, dz = DP_STEPS[k]
        return (y + dy) % NY * NZ + (z + sign * dz + NZ) % NZ

    def factor_at(k, sign=1):
        dx, dh, dc = FACTOR_STEPS[k]
        return (fx + sign * dx + 4) % 4 * 4 + (fh + dh) % 2 * 2 + (fc + dc) % 2

    bin_load = pltpu.make_async_copy(bin_hbm, bin_raw, load_sem.at[0])
    qx_load = pltpu.make_async_copy(qx_hbm.at[0], qx_raw, load_sem.at[1])
    qcot_load = pltpu.make_async_copy(qcot_hbm.at[0], qcot_raw, load_sem.at[2])
    bout_load = pltpu.make_async_copy(bout_hbm, bout, load_sem.at[3])
    eig_load = pltpu.make_async_copy(eig_hbm, eig_raw, load_sem.at[4])

    def x_load(b):
        return pltpu.make_async_copy(x_hbm.at[b], x_raw.at[b], x_sem.at[b])

    def cot_load(b):
        return pltpu.make_async_copy(cot_hbm.at[b], cot_raw.at[b], cot_sem.at[b])

    for copy in (bin_load, qx_load, qcot_load, bout_load, eig_load):
        copy.start()

    barrier = pltpu.get_barrier_semaphore()
    for k in range(ND - 1):
        pl.semaphore_signal(barrier, inc=1, device_id=(dp_at(k), f), device_id_type=MESH)
    for k in range(NF - 1):
        pl.semaphore_signal(barrier, inc=1, device_id=(d, factor_at(k)), device_id_type=MESH)
    for b in range(BATCH):
        x_load(b).start()
        cot_load(b).start()

    xl[BATCH, 0:64, :] = jnp.zeros((64, 1024), bf16)
    xl[BATCH, 576:640, :] = jnp.zeros((64, 1024), bf16)

    bin_load.wait()
    block = bin_raw[...].astype(f32)
    tail_a = block[0:96, 128:180]
    tail_b = jnp.concatenate([block[96:180, 128:180], jnp.zeros((12, 52), f32)], axis=0)
    gap = jnp.zeros((96, 12), f32)
    panels[pl.ds(d, 1), 0:192, :] = jnp.concatenate(
        [block[:, 0:128], jnp.zeros((12, 128), f32)], axis=0
    ).astype(bf16)[None]
    panels[pl.ds(d, 1), 192:288, :] = jnp.concatenate([tail_a, gap, tail_b, gap], axis=1).astype(bf16)[None]

    qx_load.wait()
    qcot_load.wait()
    fill_patches(qx_raw[...], xl, BATCH)
    query_t = qcot_raw[...].reshape(POS, CH).T
    for half in range(NY):
        number = block_of(half, jnp.minimum(f, BLOCKS - 1))
        mq[half] = jnp.dot(
            query_t,
            xl[
                BATCH,
                pl.ds(pl.multiple_of(number // 8 * 64, 64), POS),
                pl.ds(pl.multiple_of(number % 8 * 128, 128), 128),
            ],
            preferred_element_type=f32,
        )
    for part in range(ND):
        row = part % NZ * CS
        p1_src[part] = mq[part // NZ, row : row + CS, :].astype(bf16)

    def basis_copy(number):
        origin, (start, count), hop = PLAN[number]
        slot = (y + origin[0]) % NY * NZ + (z + origin[1] + NZ) % NZ
        view = panels.at[slot, pl.ds(start, count)]
        peer = (y + hop[0]) % NY * NZ + (z + hop[1] + NZ) % NZ
        return pltpu.make_async_remote_copy(
            src_ref=view, dst_ref=view, send_sem=bin_send.at[number], recv_sem=bin_recv.at[number],
            device_id=(peer, f), device_id_type=MESH,
        )

    seen = set()

    def basis_wait(origin):
        for place, number in LANDS.items():
            if place[0] != norm(origin) or place in seen:
                continue
            seen.add(place)
            start, count = place[1]
            slot = (y + place[0][0]) % NY * NZ + (z + place[0][1]) % NZ
            view = panels.at[slot, pl.ds(start, count)]
            pltpu.make_async_remote_copy(
                src_ref=view, dst_ref=view, send_sem=bin_send.at[number], recv_sem=bin_recv.at[number],
                device_id=(d, f), device_id_type=MESH,
            ).wait_recv()

    def basis_forward(copies):
        for copy in copies:
            basis_wait(copy[0])
            basis_copy(PLAN.index(copy)).start()

    def to_dp(k, src, dst, send, recv):
        return pltpu.make_async_remote_copy(
            src_ref=src, dst_ref=dst, send_sem=send.at[k], recv_sem=recv.at[k],
            device_id=(dp_at(k), f), device_id_type=MESH,
        )

    def to_factor(k, src, dst, send, recv):
        return pltpu.make_async_remote_copy(
            src_ref=src, dst_ref=dst, send_sem=send.at[k], recv_sem=recv.at[k],
            device_id=(d, factor_at(k)), device_id_type=MESH,
        )

    def p1_copy(k):
        return to_dp(k, p1_src.at[dp_at(k)], p1_dst.at[d], p1_send, p1_recv)

    def p1_land(k):
        sender = dp_at(k, -1)
        return to_dp(k, p1_src.at[sender], p1_dst.at[sender], p1_send, p1_recv)

    def p2_copy(k):
        return to_factor(k, p2_buf.at[f], p2_buf.at[f], p2_send, p2_recv)

    def p2_land(k):
        sender = factor_at(k, -1)
        return sender, to_factor(k, p2_buf.at[sender], p2_buf.at[sender], p2_send, p2_recv)

    def ag_copy(k):
        return to_dp(k, ag_buf.at[d], ag_buf.at[d], ag_send, ag_recv)

    def ag_land(k):
        sender = dp_at(k, -1)
        return to_dp(k, ag_buf.at[sender], ag_buf.at[sender], ag_send, ag_recv)

    def ar_copy(k):
        return to_factor(k, ar_buf.at[f], ar_buf.at[f], ar_send, ar_recv)

    def ar_land(k):
        sender = factor_at(k, -1)
        return to_factor(k, ar_buf.at[sender], ar_buf.at[sender], ar_send, ar_recv)

    pl.semaphore_wait(barrier, ND + NF - 2)

    @pl.when(f < BLOCKS)
    def _():
        for k in range(ND - 1):
            p1_copy(k).start()

    for number in range(len(START)):
        basis_copy(number).start()

    p1_dst[pl.ds(d, 1)] = p1_src[pl.ds(d, 1)]

    flat[:, 128:256] = jnp.zeros((9 * CH, 128), f32)
    panel[...] = jnp.zeros_like(panel)
    q_pad[...] = jnp.zeros_like(q_pad)
    bout_load.wait()
    bout_t[...] = bout[...].T
    eig_load.wait()
    scale[...] = (1.0 / 16) / (eig_raw[...].T + damping)

    def prepare(b, carry):
        x_load(b).wait()
        cot_load(b).wait()
        xl[b, 0:64, :] = jnp.zeros((64, 1024), bf16)
        xl[b, 576:640, :] = jnp.zeros((64, 1024), bf16)
        fill_patches(x_raw[b], xl, b)
        rotated_cot = jnp.dot(cot_raw[b].reshape(POS, CH), bout[...], preferred_element_type=f32)
        r_all[b] = rotated_cot.astype(bf16).T
        return carry

    lax.fori_loop(0, PREPARED, prepare, 0)

    @pl.when(f < BLOCKS)
    def _():
        for k in range(ND - 1):
            p1_land(k).wait_recv()
        total = p1_dst[0].astype(f32)
        for part in range(1, ND):
            total += p1_dst[part].astype(f32)
        p2_buf[pl.ds(f, 1)] = total[None]
        for k in range(NF - 1):
            p2_copy(k).start()

    basis_forward(COLUMN)
    basis_forward(ACROSS_NEAR)
    lax.fori_loop(PREPARED, BATCH, prepare, 0)
    basis_forward(ACROSS_FAR)

    def unpack(half, goal_panel):
        for part in range(half * NZ, half * NZ + NZ):
            row = part * SIDE
            flat[row : row + SIDE, 0:128] = panels[part, 0:SIDE, :].astype(f32)
            tails = panels[part, 192:288, :].astype(f32)
            turned = pltpu.roll(tails, 64, 1)
            flat[row : row + 96, 128:192] = tails[:, 0:64]
            flat[row + 96 : row + SIDE, 128:192] = turned[0 : SIDE - 96, 0:64]
        low, high = half * NZ * SIDE, (half + 1) * NZ * SIDE
        for tap in range(9):
            tap_row, tap_col = tap // 3, tap % 3
            for begin, size, goal in (
                (0, 256, tap_row * 1024 + tap_col * 256),
                (256, 64, tap_row * 1024 + 768 + tap_col * 64),
            ):
                first = max(tap * CH + begin, low)
                last = min(tap * CH + begin + size, high)
                if first < last:
                    goal += first - tap * CH - begin
                    panel[goal_panel, goal : goal + last - first, :] = flat[first:last, :].astype(bf16)

    for half in range(NY):

        @pl.when(y == half)
        def _():
            unpack(half, 0)

    for k in range(NF - 1):
        sender, landing = p2_land(k)

        @pl.when(sender < BLOCKS)
        def _():
            landing.wait_recv()

    for part in range(BLOCKS):
        rows = p2_buf[part]
        high = rows.astype(bf16)
        m_stack[0:CS, part * 128 : (part + 1) * 128] = high
        m_stack[48 : 48 + CS, part * 128 : (part + 1) * 128] = (rows - high.astype(f32)).astype(bf16)
    main_rows = pl.ds(pl.multiple_of(y * (11 * 128), 128), 12 * 128)
    last_rows = pl.ds(pl.multiple_of((14 + 9 * y) * 128, 128), 128)
    both_v = jnp.dot(m_stack[:, : 12 * 128], panel[0, main_rows, :], preferred_element_type=f32) + jnp.dot(
        m_stack[:, 12 * 128 :], panel[0, last_rows, :], preferred_element_type=f32
    )
    part_v = both_v[0:CS] + both_v[48 : 48 + CS]
    tail_v = jnp.concatenate(
        [part_v[0:24, 128:192], jnp.concatenate([part_v[24:40, 128:192], jnp.zeros((8, 64), f32)], axis=0)],
        axis=1,
    )
    ag_buf[pl.ds(d, 1)] = jnp.concatenate([part_v[:, 0:128], tail_v], axis=0).astype(bf16)[None]
    for k in range(ND - 1):
        ag_copy(k).start()

    def half_product(b, half, which):
        line = pl.multiple_of(half * 128, 128)
        whole = jnp.dot(
            xl[b, pl.ds(line, POS), :],
            panel[which, pl.ds(pl.multiple_of(half * 2048, 2048), 1024), :],
            preferred_element_type=f32,
        )
        start = pl.multiple_of(half * 384, 128)
        whole += jnp.dot(
            xl[b, 64 : 64 + POS, pl.ds(start, 512)],
            panel[which, pl.ds(pl.multiple_of(1024 + half * 384, 128), 512), :],
            preferred_element_type=f32,
        )
        last = pl.multiple_of(768 + half * 128, 128)
        whole += jnp.dot(
            xl[b, 64 : 64 + POS, pl.ds(last, 128)],
            panel[which, pl.ds(pl.multiple_of(1792 + half * 128, 128), 128), :],
            preferred_element_type=f32,
        )
        return whole

    def first_half(b, carry):
        acc[b] = half_product(b, y, 0)
        return carry

    lax.fori_loop(0, BATCH, first_half, 0)

    for place in LANDS:
        basis_wait(place[0])
    for half in range(NY):

        @pl.when(y != half)
        def _():
            unpack(half, 1)

    def second_half(b, carry):
        proj = (acc[b] + half_product(b, 1 - y, 1)).astype(bf16)
        w_all[b] = jnp.dot(r_all[b], proj, preferred_element_type=f32)
        return carry

    lax.fori_loop(0, BATCH, second_half, 0)

    for k in range(ND - 1):
        ag_land(k).wait_recv()
    for part in range(NZ):
        both = ag_buf[part].astype(f32) + ag_buf[NZ + part].astype(f32)
        row = part * CS
        v_flat[row : row + CS, 0:128] = both[0:40]
        tails = both[40:64]
        turned = pltpu.roll(tails, 64, 1)
        half_line = lax.broadcasted_iota(jnp.int32, (24, 128), 1) < 64
        v_flat[row : row + 24, 128:256] = jnp.where(half_line, tails, 0.0)
        v_flat[row + 24 : row + CS, 128:256] = jnp.where(half_line, turned, 0.0)[0:16]
    v_full = v_flat[...]
    v_high = v_full.astype(bf16)
    v_low = (v_full - v_high.astype(f32)).astype(bf16)
    rotated = jnp.dot(bout_t[...], v_high, preferred_element_type=f32) + jnp.dot(
        bout_t[...], v_low, preferred_element_type=f32
    )
    q_pad[:, :SIDE] = rotated[:, :SIDE] * scale[...]
    q_full = q_pad[...]
    sums = []
    for b in range(BATCH):
        line = jnp.sum(w_all[b] * q_full, axis=0, keepdims=True)
        sums.append(line[:, :128] + line[:, 128:])
    ar_buf[pl.ds(f, 1)] = jnp.concatenate(sums, axis=0)[None]
    for k in range(NF - 1):
        ar_copy(k).start()

    proj_out[...] = q_pad[...].T[:SIDE, :]
    proj_store = pltpu.make_async_copy(proj_out, proj_hbm, load_sem.at[5])
    proj_store.start()
    phase = (time_ref[...].astype(f32) / 1000.0 + 0.008) / 1.008 * (math.pi / 2)
    weight = jnp.sin(phase) / math.sqrt(CH * CH * 9)
    for number in range(len(PLAN)):
        basis_copy(number).wait_send()

    @pl.when(f < BLOCKS)
    def _():
        for k in range(ND - 1):
            p1_copy(k).wait_send()
        for k in range(NF - 1):
            p2_copy(k).wait_send()

    for k in range(ND - 1):
        ag_copy(k).wait_send()

    for k in range(NF - 1):
        ar_land(k).wait_recv()
    total = ar_buf[0]
    for part in range(1, NF):
        total += ar_buf[part]
    score = jnp.broadcast_to(jnp.sum(total, axis=1, keepdims=True), (BATCH, 128))
    at = lax.broadcasted_iota(jnp.int32, (BATCH, 128), 0) == lax.broadcasted_iota(jnp.int32, (BATCH, 128), 1)
    score_ref[...] = jnp.sum(jnp.where(at, score, 0.0), axis=0, keepdims=True)[:, :BATCH] * weight
    proj_store.wait()
    for k in range(NF - 1):
        ar_copy(k).wait_send()


def on_device(x, cot, qx, qcot, timesteps, basis, bout, eig):
    hbm = pl.BlockSpec(memory_space=pl.ANY)
    vmem = pl.BlockSpec(memory_space=pltpu.VMEM)
    dma = pltpu.SemaphoreType.DMA
    raw, query_proj = pl.pallas_call(
        kernel,
        out_shape=(
            jax.ShapeDtypeStruct((1, BATCH), f32),
            jax.ShapeDtypeStruct((SIDE, CH), f32),
        ),
        in_specs=[hbm] * 7 + [vmem],
        out_specs=(vmem, hbm),
        scratch_shapes=[
            pltpu.VMEM((BATCH, 8, 64, CH), bf16),
            pltpu.VMEM((BATCH, 8, 64, CH), bf16),
            pltpu.VMEM((8, 64, CH), bf16),
            pltpu.VMEM((8, 64, CH), bf16),
            pltpu.VMEM((SIDE, SIDE), bf16),
            pltpu.VMEM((CH, CH), bf16),
            pltpu.VMEM((CH, CH), bf16),
            pltpu.VMEM((SIDE, CH), f32),
            pltpu.VMEM((CH, SIDE), f32),
            pltpu.VMEM((ND, PACK, 128), bf16),
            pltpu.VMEM((9 * CH, 256), f32),
            pltpu.VMEM((2, 3072, 256), bf16),
            pltpu.VMEM((BATCH + 1, 640, 1024), bf16),
            pltpu.VMEM((BATCH, CH, POS), bf16),
            pltpu.VMEM((BATCH, POS, 256), f32),
            pltpu.VMEM((BATCH, CH, 256), f32),
            pltpu.VMEM((SIDE, CH), f32),
            pltpu.VMEM((NY, CH, 128), f32),
            pltpu.VMEM((ND, CS, 128), bf16),
            pltpu.VMEM((ND, CS, 128), bf16),
            pltpu.VMEM((NF, CS, 128), f32),
            pltpu.VMEM((96, BLOCKS * 128), bf16),
            pltpu.VMEM((ND, 64, 128), bf16),
            pltpu.VMEM((CH, 256), f32),
            pltpu.VMEM((CH, 256), f32),
            pltpu.VMEM((NF, BATCH, 128), f32),
            dma((6,)),
            dma((BATCH,)),
            dma((BATCH,)),
            dma((len(PLAN),)),
            dma((len(PLAN),)),
            dma((ND,)),
            dma((ND,)),
            dma((NF,)),
            dma((NF,)),
            dma((ND,)),
            dma((ND,)),
            dma((NF,)),
            dma((NF,)),
        ],
        compiler_params=pltpu.CompilerParams(
            collective_id=0, has_side_effects=True, vmem_limit_bytes=58 * 1024 * 1024
        ),
        name="influence",
    )(x, cot, qx, qcot, basis, bout, eig.T, timesteps[None])
    return raw[0], query_proj.T


def solution(mesh):
    in_specs = (
        P("dp", None, None, None),
        P("dp", None, None, None),
        P("dp", None, None, None),
        P("dp", None, None, None),
        P("dp"),
        P("dp", "factor"),
        P(),
        P(None, "factor"),
    )
    out_specs = (P("dp"), P(None, "factor"))
    return jax.shard_map(
        on_device, mesh=mesh, in_specs=in_specs, out_specs=out_specs, check_vma=False
    )
```

```python
import functools
import math

import jax
import jax.numpy as jnp
from jax import lax
from jax.experimental import pallas as pl
from jax.experimental.pallas import tpu as pltpu
from jax.sharding import PartitionSpec as P

damping = 0.01
MESH = pl.DeviceIdType.MESH
bf16 = jnp.bfloat16
f32 = jnp.float32

NY, NZ = 2, 8
ND, NF = 16, 16
CH = 320
SIDE = 180
CS = 40
BLOCKS = 12
HALF = 1536
POS = 512
BATCH = 8
PREPARED = 5
PACK = 288

WHOLE, HALF_A, HALF_B = (0, 288), (0, 144), (144, 144)


def norm(origin):
    return (origin[0] % NY, origin[1] % NZ)


START = [
    ((0, 0), WHOLE, (0, 2)), ((0, 0), WHOLE, (0, -2)),
    ((0, 0), WHOLE, (0, 1)), ((0, 0), WHOLE, (0, -1)),
    ((0, 0), WHOLE, (1, 0)),
]
COLUMN = [
    ((0, -2), HALF_A, (0, 2)), ((0, 2), HALF_B, (0, -2)),
    ((0, -2), WHOLE, (0, 1)), ((0, 2), WHOLE, (0, -1)),
]
ACROSS_NEAR = [((1, 0), WHOLE, (0, k)) for k in (1, -1)] + [((0, k), WHOLE, (1, 0)) for k in (2, -2)]
ACROSS_FAR = [((0, k), WHOLE, (1, 0)) for k in (3, -3, 4)]
PLAN = START + COLUMN + ACROSS_NEAR + ACROSS_FAR
LANDS = {}
for number, (origin, rows, hop) in enumerate(PLAN):
    place = (norm((origin[0] - hop[0], origin[1] - hop[1])), rows)
    assert place not in LANDS
    LANDS[place] = number


DP_STEPS = sorted(
    ((dy, dz) for dy in range(NY) for dz in range(NZ) if dy or dz),
    key=lambda step: -(step[0] + min(step[1], NZ - step[1])),
)
FACTOR_STEPS = sorted(
    ((dx, dh, dc) for dx in range(4) for dh in range(2) for dc in range(2) if dx or dh or dc),
    key=lambda step: -(min(step[0], 4 - step[0]) + 2 * step[1] + 0.1 * step[2]),
)


def fill_patches(raw, xl, slot):
    x = raw.reshape(POS, CH).astype(f32)
    col = lax.broadcasted_iota(jnp.int32, (POS, 1), 0) % 64
    main = x[:, :256]
    rest = jnp.concatenate([x[:, 256:], jnp.zeros((POS, 64), f32)], axis=1)
    pad = jnp.zeros((POS, 32), f32)

    def left(v):
        return jnp.where(col == 0, 0.0, pltpu.roll(v, 1, 0))

    def right(v):
        return jnp.where(col == 63, 0.0, pltpu.roll(v, POS - 1, 0))

    inside = pl.ds(64, POS)
    xl[slot, inside, 0:256] = left(main).astype(bf16)
    xl[slot, inside, 256:512] = jnp.concatenate([left(rest)[:, :64], x[:, 0:160], pad], axis=1).astype(bf16)
    xl[slot, inside, 512:768] = right(main).astype(bf16)
    xl[slot, inside, 768:1024] = jnp.concatenate([right(rest)[:, :64], x[:, 160:320], pad], axis=1).astype(bf16)


LAYOUT = (
    ((0, 256, 0), (256, 320, 256)),
    ((0, 160, 320), (160, 320, 832)),
    ((0, 256, 512), (256, 320, 768)),
)


def kernel(
    x_hbm, cot_hbm, qx_hbm, qcot_hbm, bin_hbm, bout_hbm, eig_hbm, time_ref,
    score_ref, proj_hbm,
    x_raw, cot_raw, qx_raw, qcot_raw, bin_raw, bout, bout_t, eig_raw, scale,
    panels, flat, panel, xl, r_all, acc, proj_all, w_all, proj_out,
    mq, p1_src, p1_dst, p2_buf, m_stack, ag_buf, v_flat, q_pad, ar_buf,
    load_sem, x_sem, cot_sem,
    bin_send, bin_recv, p1_send, p1_recv, p2_send, p2_recv, ag_send, ag_recv, ar_send, ar_recv,
):
    d = lax.axis_index("dp")
    f = lax.axis_index("factor")
    y, z = d // NZ, d % NZ
    fx, fh, fc = f // 4, f // 2 % 2, f % 2

    def dp_at(k, sign=1):
        dy, dz = DP_STEPS[k]
        return (y + dy) % NY * NZ + (z + sign * dz + NZ) % NZ

    def factor_at(k, sign=1):
        dx, dh, dc = FACTOR_STEPS[k]
        return (fx + sign * dx + 4) % 4 * 4 + (fh + dh) % 2 * 2 + (fc + dc) % 2

    bin_load = pltpu.make_async_copy(bin_hbm, bin_raw, load_sem.at[0])
    qx_load = pltpu.make_async_copy(qx_hbm.at[0], qx_raw, load_sem.at[1])
    qcot_load = pltpu.make_async_copy(qcot_hbm.at[0], qcot_raw, load_sem.at[2])
    bout_load = pltpu.make_async_copy(bout_hbm, bout, load_sem.at[3])
    eig_load = pltpu.make_async_copy(eig_hbm, eig_raw, load_sem.at[4])

    def x_load(b):
        return pltpu.make_async_copy(x_hbm.at[b], x_raw.at[b], x_sem.at[b])

    def cot_load(b):
        return pltpu.make_async_copy(cot_hbm.at[b], cot_raw.at[b], cot_sem.at[b])

    for copy in (bin_load, qx_load, qcot_load, bout_load, eig_load):
        copy.start()

    barrier = pltpu.get_barrier_semaphore()
    for k in range(ND - 1):
        pl.semaphore_signal(barrier, inc=1, device_id=(dp_at(k), f), device_id_type=MESH)
    for k in range(NF - 1):
        pl.semaphore_signal(barrier, inc=1, device_id=(d, factor_at(k)), device_id_type=MESH)
    for b in range(BATCH):
        x_load(b).start()
        cot_load(b).start()

    xl[BATCH, 0:64, :] = jnp.zeros((64, 1024), bf16)
    xl[BATCH, 576:640, :] = jnp.zeros((64, 1024), bf16)

    qx_load.wait()
    qcot_load.wait()
    fill_patches(qx_raw[...], xl, BATCH)
    query_t = qcot_raw[...].reshape(POS, CH).T
    for half in range(NY):
        number = half * BLOCKS + jnp.minimum(f, BLOCKS - 1)
        mq[half] = jnp.dot(
            query_t,
            xl[
                BATCH,
                pl.ds(pl.multiple_of(number // 8 * 64, 64), POS),
                pl.ds(pl.multiple_of(number % 8 * 128, 128), 128),
            ],
            preferred_element_type=f32,
        )
    for part in range(ND):
        row = part % NZ * CS
        p1_src[part] = mq[part // NZ, row : row + CS, :].astype(bf16)

    def basis_copy(number):
        origin, (start, count), hop = PLAN[number]
        slot = (y + origin[0]) % NY * NZ + (z + origin[1] + NZ) % NZ
        view = panels.at[slot, pl.ds(start, count)]
        peer = (y + hop[0]) % NY * NZ + (z + hop[1] + NZ) % NZ
        return pltpu.make_async_remote_copy(
            src_ref=view, dst_ref=view, send_sem=bin_send.at[number], recv_sem=bin_recv.at[number],
            device_id=(peer, f), device_id_type=MESH,
        )

    seen = set()

    def basis_wait(origin):
        for place, number in LANDS.items():
            if place[0] != norm(origin) or place in seen:
                continue
            seen.add(place)
            start, count = place[1]
            slot = (y + place[0][0]) % NY * NZ + (z + place[0][1]) % NZ
            view = panels.at[slot, pl.ds(start, count)]
            pltpu.make_async_remote_copy(
                src_ref=view, dst_ref=view, send_sem=bin_send.at[number], recv_sem=bin_recv.at[number],
                device_id=(d, f), device_id_type=MESH,
            ).wait_recv()

    def basis_forward(copies):
        for copy in copies:
            basis_wait(copy[0])
            basis_copy(PLAN.index(copy)).start()

    def to_dp(k, src, dst, send, recv):
        return pltpu.make_async_remote_copy(
            src_ref=src, dst_ref=dst, send_sem=send.at[k], recv_sem=recv.at[k],
            device_id=(dp_at(k), f), device_id_type=MESH,
        )

    def to_factor(k, src, dst, send, recv):
        return pltpu.make_async_remote_copy(
            src_ref=src, dst_ref=dst, send_sem=send.at[k], recv_sem=recv.at[k],
            device_id=(d, factor_at(k)), device_id_type=MESH,
        )

    def p1_copy(k):
        return to_dp(k, p1_src.at[dp_at(k)], p1_dst.at[d], p1_send, p1_recv)

    def p1_land(k):
        sender = dp_at(k, -1)
        return to_dp(k, p1_src.at[sender], p1_dst.at[sender], p1_send, p1_recv)

    def p2_copy(k):
        return to_factor(k, p2_buf.at[f], p2_buf.at[f], p2_send, p2_recv)

    def p2_land(k):
        sender = factor_at(k, -1)
        return sender, to_factor(k, p2_buf.at[sender], p2_buf.at[sender], p2_send, p2_recv)

    def ag_copy(k):
        return to_dp(k, ag_buf.at[d], ag_buf.at[d], ag_send, ag_recv)

    def ag_land(k):
        sender = dp_at(k, -1)
        return to_dp(k, ag_buf.at[sender], ag_buf.at[sender], ag_send, ag_recv)

    def ar_copy(k):
        return to_factor(k, ar_buf.at[f], ar_buf.at[f], ar_send, ar_recv)

    def ar_land(k):
        sender = factor_at(k, -1)
        return to_factor(k, ar_buf.at[sender], ar_buf.at[sender], ar_send, ar_recv)

    pl.semaphore_wait(barrier, ND + NF - 2)

    @pl.when(f < BLOCKS)
    def _():
        for k in range(ND - 1):
            p1_copy(k).start()

    bin_load.wait()
    block = bin_raw[...].astype(f32)
    tail_a = block[0:96, 128:180]
    tail_b = jnp.concatenate([block[96:180, 128:180], jnp.zeros((12, 52), f32)], axis=0)
    gap = jnp.zeros((96, 12), f32)
    panels[pl.ds(d, 1), 0:192, :] = jnp.concatenate(
        [block[:, 0:128], jnp.zeros((12, 128), f32)], axis=0
    ).astype(bf16)[None]
    panels[pl.ds(d, 1), 192:288, :] = jnp.concatenate([tail_a, gap, tail_b, gap], axis=1).astype(bf16)[None]

    for number in range(len(START)):
        basis_copy(number).start()

    p1_dst[pl.ds(d, 1)] = p1_src[pl.ds(d, 1)]

    flat[:, 128:256] = jnp.zeros((9 * CH, 128), f32)
    panel[...] = jnp.zeros_like(panel)
    q_pad[...] = jnp.zeros_like(q_pad)
    bout_load.wait()
    bout_t[...] = bout[...].T
    eig_load.wait()
    scale[...] = (1.0 / 16) / (eig_raw[...].T + damping)

    def prepare(b, carry):
        x_load(b).wait()
        cot_load(b).wait()
        xl[b, 0:64, :] = jnp.zeros((64, 1024), bf16)
        xl[b, 576:640, :] = jnp.zeros((64, 1024), bf16)
        fill_patches(x_raw[b], xl, b)
        rotated_cot = jnp.dot(cot_raw[b].reshape(POS, CH), bout[...], preferred_element_type=f32)
        r_all[b] = rotated_cot.astype(bf16).T
        return carry

    lax.fori_loop(0, PREPARED, prepare, 0)

    @pl.when(f < BLOCKS)
    def _():
        for k in range(ND - 1):
            p1_land(k).wait_recv()
        total = p1_dst[0].astype(f32)
        for part in range(1, ND):
            total += p1_dst[part].astype(f32)
        p2_buf[pl.ds(f, 1)] = total[None]
        for k in range(NF - 1):
            p2_copy(k).start()

    basis_forward(COLUMN)
    basis_forward(ACROSS_NEAR)
    lax.fori_loop(PREPARED, BATCH, prepare, 0)
    basis_forward(ACROSS_FAR)

    def unpack(half):
        for part in range(half * NZ, half * NZ + NZ):
            row = part * SIDE
            flat[row : row + SIDE, 0:128] = panels[part, 0:SIDE, :].astype(f32)
            tails = panels[part, 192:288, :].astype(f32)
            turned = pltpu.roll(tails, 64, 1)
            flat[row : row + 96, 128:192] = tails[:, 0:64]
            flat[row + 96 : row + SIDE, 128:192] = turned[0 : SIDE - 96, 0:64]
        low, high = half * NZ * SIDE, (half + 1) * NZ * SIDE
        for tap in range(9):
            tap_row, tap_col = tap // 3, tap % 3
            for begin, end, goal in LAYOUT[tap_col]:
                first = max(tap * CH + begin, low)
                last = min(tap * CH + end, high)
                if first < last:
                    goal += tap_row * 1024 + first - tap * CH - begin
                    panel[goal : goal + last - first, :] = flat[first:last, :].astype(bf16)

    for k in range(1, NZ):
        basis_wait((0, k))
    for half in range(NY):

        @pl.when(y == half)
        def _():
            unpack(half)

    for k in range(NF - 1):
        sender, landing = p2_land(k)

        @pl.when(sender < BLOCKS)
        def _():
            landing.wait_recv()

    for part in range(BLOCKS):
        rows = p2_buf[part]
        high = rows.astype(bf16)
        m_stack[0:CS, part * 128 : (part + 1) * 128] = high
        m_stack[48 : 48 + CS, part * 128 : (part + 1) * 128] = (rows - high.astype(f32)).astype(bf16)
    own_rows = pl.ds(pl.multiple_of(y * HALF, HALF), HALF)
    both_v = jnp.dot(m_stack[...], panel[own_rows, :], preferred_element_type=f32)
    part_v = both_v[0:CS] + both_v[48 : 48 + CS]
    tail_v = jnp.concatenate(
        [part_v[0:24, 128:192], jnp.concatenate([part_v[24:40, 128:192], jnp.zeros((8, 64), f32)], axis=0)],
        axis=1,
    )
    ag_buf[pl.ds(d, 1)] = jnp.concatenate([part_v[:, 0:128], tail_v], axis=0).astype(bf16)[None]
    for k in range(ND - 1):
        ag_copy(k).start()

    def half_product(b, half):
        whole_row = jnp.dot(
            xl[b, pl.ds(pl.multiple_of(half * 128, 128), POS), :],
            panel[pl.ds(pl.multiple_of(half * 2048, 2048), 1024), :],
            preferred_element_type=f32,
        )
        return whole_row + jnp.dot(
            xl[b, 64 : 64 + POS, pl.ds(pl.multiple_of(half * 512, 512), 512)],
            panel[pl.ds(pl.multiple_of(1024 + half * 512, 512), 512), :],
            preferred_element_type=f32,
        )

    def first_half(b, carry):
        acc[b] = half_product(b, y)
        return carry

    lax.fori_loop(0, BATCH, first_half, 0)

    for place in LANDS:
        basis_wait(place[0])
    for half in range(NY):

        @pl.when(y != half)
        def _():
            unpack(half)

    def second_half(b, carry):
        proj_all[b] = (acc[b] + half_product(b, 1 - y)).astype(bf16)
        return carry

    lax.fori_loop(0, BATCH, second_half, 0)

    def contract(b, carry):
        w_all[b] = jnp.dot(r_all[b], proj_all[b], preferred_element_type=f32)
        return carry

    lax.fori_loop(0, BATCH, contract, 0, unroll=2)

    for k in range(ND - 1):
        ag_land(k).wait_recv()
    for part in range(NZ):
        both = ag_buf[part].astype(f32) + ag_buf[NZ + part].astype(f32)
        row = part * CS
        v_flat[row : row + CS, 0:128] = both[0:40]
        tails = both[40:64]
        turned = pltpu.roll(tails, 64, 1)
        half_line = lax.broadcasted_iota(jnp.int32, (24, 128), 1) < 64
        v_flat[row : row + 24, 128:256] = jnp.where(half_line, tails, 0.0)
        v_flat[row + 24 : row + CS, 128:256] = jnp.where(half_line, turned, 0.0)[0:16]
    v_full = v_flat[...]
    v_high = v_full.astype(bf16)
    v_low = (v_full - v_high.astype(f32)).astype(bf16)
    rotated = jnp.dot(bout_t[...], v_high, preferred_element_type=f32) + jnp.dot(
        bout_t[...], v_low, preferred_element_type=f32
    )
    q_pad[:, :SIDE] = rotated[:, :SIDE] * scale[...]
    q_full = q_pad[...]
    sums = []
    for b in range(BATCH):
        line = jnp.sum(w_all[b] * q_full, axis=0, keepdims=True)
        sums.append(line[:, :128] + line[:, 128:])
    ar_buf[pl.ds(f, 1)] = jnp.concatenate(sums, axis=0)[None]
    for k in range(NF - 1):
        ar_copy(k).start()

    proj_out[...] = q_pad[...].T[:SIDE, :]
    proj_store = pltpu.make_async_copy(proj_out, proj_hbm, load_sem.at[5])
    proj_store.start()
    phase = (time_ref[...].astype(f32) / 1000.0 + 0.008) / 1.008 * (math.pi / 2)
    weight = jnp.sin(phase) / math.sqrt(CH * CH * 9)
    for number in range(len(PLAN)):
        basis_copy(number).wait_send()

    @pl.when(f < BLOCKS)
    def _():
        for k in range(ND - 1):
            p1_copy(k).wait_send()
        for k in range(NF - 1):
            p2_copy(k).wait_send()

    for k in range(ND - 1):
        ag_copy(k).wait_send()

    for k in range(NF - 1):
        ar_land(k).wait_recv()
    total = ar_buf[0]
    for part in range(1, NF):
        total += ar_buf[part]
    score = jnp.broadcast_to(jnp.sum(total, axis=1, keepdims=True), (BATCH, 128))
    at = lax.broadcasted_iota(jnp.int32, (BATCH, 128), 0) == lax.broadcasted_iota(jnp.int32, (BATCH, 128), 1)
    score_ref[...] = jnp.sum(jnp.where(at, score, 0.0), axis=0, keepdims=True)[:, :BATCH] * weight
    proj_store.wait()
    for k in range(NF - 1):
        ar_copy(k).wait_send()


def finish(raw_ref, proj_ref, score_ref, out_ref):
    score_ref[...] = raw_ref[...]
    out_ref[...] = proj_ref[...]


def on_device(x, cot, qx, qcot, timesteps, basis, bout, eig):
    hbm = pl.BlockSpec(memory_space=pl.ANY)
    vmem = pl.BlockSpec(memory_space=pltpu.VMEM)
    dma = pltpu.SemaphoreType.DMA
    raw, query_proj = pl.pallas_call(
        kernel,
        out_shape=(
            jax.ShapeDtypeStruct((1, BATCH), f32),
            jax.ShapeDtypeStruct((SIDE, CH), f32),
        ),
        in_specs=[hbm] * 7 + [vmem],
        out_specs=(vmem, hbm),
        scratch_shapes=[
            pltpu.VMEM((BATCH, 8, 64, CH), bf16),
            pltpu.VMEM((BATCH, 8, 64, CH), bf16),
            pltpu.VMEM((8, 64, CH), bf16),
            pltpu.VMEM((8, 64, CH), bf16),
            pltpu.VMEM((SIDE, SIDE), bf16),
            pltpu.VMEM((CH, CH), bf16),
            pltpu.VMEM((CH, CH), bf16),
            pltpu.VMEM((SIDE, CH), f32),
            pltpu.VMEM((CH, SIDE), f32),
            pltpu.VMEM((ND, PACK, 128), bf16),
            pltpu.VMEM((9 * CH, 256), f32),
            pltpu.VMEM((2 * HALF, 256), bf16),
            pltpu.VMEM((BATCH + 1, 640, 1024), bf16),
            pltpu.VMEM((BATCH, CH, POS), bf16),
            pltpu.VMEM((BATCH, POS, 256), f32),
            pltpu.VMEM((BATCH, POS, 256), bf16),
            pltpu.VMEM((BATCH, CH, 256), f32),
            pltpu.VMEM((SIDE, CH), f32),
            pltpu.VMEM((NY, CH, 128), f32),
            pltpu.VMEM((ND, CS, 128), bf16),
            pltpu.VMEM((ND, CS, 128), bf16),
            pltpu.VMEM((NF, CS, 128), f32),
            pltpu.VMEM((96, BLOCKS * 128), bf16),
            pltpu.VMEM((ND, 64, 128), bf16),
            pltpu.VMEM((CH, 256), f32),
            pltpu.VMEM((CH, 256), f32),
            pltpu.VMEM((NF, BATCH, 128), f32),
            dma((6,)),
            dma((BATCH,)),
            dma((BATCH,)),
            dma((len(PLAN),)),
            dma((len(PLAN),)),
            dma((ND,)),
            dma((ND,)),
            dma((NF,)),
            dma((NF,)),
            dma((ND,)),
            dma((ND,)),
            dma((NF,)),
            dma((NF,)),
        ],
        compiler_params=pltpu.CompilerParams(
            collective_id=0, has_side_effects=True, vmem_limit_bytes=58 * 1024 * 1024
        ),
        name="influence",
    )(x, cot, qx, qcot, basis, bout, eig.T, timesteps[None])
    scores, query_proj = pl.pallas_call(
        finish,
        out_shape=(
            jax.ShapeDtypeStruct((1, BATCH), f32),
            jax.ShapeDtypeStruct((SIDE, CH), f32),
        ),
        in_specs=[vmem, vmem],
        out_specs=(vmem, vmem),
        name="finish",
    )(raw, query_proj)
    return scores[0], query_proj.T


def solution(mesh):
    in_specs = (
        P("dp", None, None, None),
        P("dp", None, None, None),
        P("dp", None, None, None),
        P("dp", None, None, None),
        P("dp"),
        P("dp", "factor"),
        P(),
        P(None, "factor"),
    )
    out_specs = (P("dp"), P(None, "factor"))
    return jax.shard_map(
        on_device, mesh=mesh, in_specs=in_specs, out_specs=out_specs, check_vma=False
    )
```
